256 devices in a mesh: row: 8 (over z), col: 32 (over x, y, core).
Axes of the slice: x: 4, y: 4, z: 8, core: 2. Of those that a mesh axis runs over, the one named last changes fastest.
Arguments:
- block_input: bfloat16 [1024, 8192], P('col', 'row'), may hold values from -6 to 6
- output_grad: bfloat16 [1024, 8192], P('col', 'row'), may hold values from -1.5 to 1.5
- gate_pre: bfloat16 [1024, 28672], P('row', 'col'), may hold values from -6 to 6
- up_pre: bfloat16 [1024, 28672], P('row', 'col'), may hold values from -6 to 6
- w_gate: bfloat16 [8192, 28672], P('row', 'col'), may hold values from -0.0625 to 0.0625
- w_up: bfloat16 [8192, 28672], P('row', 'col'), may hold values from -0.0625 to 0.0625
- w_down: bfloat16 [28672, 8192], P('col', 'row'), may hold values from -0.03125 to 0.03125
Outputs:
- grad_input: bfloat16 [1024, 8192], P('col', 'row')
- grad_gate: bfloat16 [8192, 28672], P('row', 'col')
- grad_up: bfloat16 [8192, 28672], P('row', 'col')
- grad_down: bfloat16 [28672, 8192], P('col', 'row')
The draws below stay inside these ranges and needn't reach their ends.
All inputs are finite; a program needn't handle non-finite values.
Results may differ from the reference program's by a relative error of at most 0.027.
Values may be sent and summed in bfloat16 or wider, within the bound.
A program may use at most 64 MiB of HBM per device.

```python
import jax
import jax.numpy as jnp
from jax import lax

D = 8192
FF = 28672
TOKENS = 1024
N_ROW = 8


def block_scale(key, dims, pieces, low, high):
    def one(position, blocks):
        draws = jax.random.uniform(jax.random.fold_in(jax.random.fold_in(key, 6), position), (blocks,), jnp.float32, low / len(pieces), high / len(pieces))
        return jnp.repeat(jnp.exp(draws), dims[position] // blocks).reshape((-1,) + (1,) * (len(dims) - position - 1))

    loudness = one(*pieces[0])
    for cut in pieces[1:]:
        loudness = loudness * one(*cut)
    return loudness


def gaussian(key, shape, width, limit, pieces=(), kind=jnp.bfloat16):
    drawn = width * jax.random.normal(key, shape, jnp.float32)
    if pieces:
        drawn = drawn * block_scale(key, shape, pieces, -0.22, 0.18)
    return jnp.clip(drawn, -limit, limit).astype(kind)


def setup_inputs(seed: int = 0) -> dict:
    seeds = jax.random.split(jax.random.key(seed), 8)
    block_input = gaussian(seeds[0], (TOKENS, D), 1.0, 6.0, ((0, 32), (1, 8)))
    output_grad = gaussian(seeds[1], (TOKENS, D), 0.25, 1.5, ((0, 32), (1, 8)))
    gate_pre = gaussian(seeds[2], (TOKENS, FF), 1.0, 6.0, ((0, 8), (1, 32)))
    up_pre = gaussian(seeds[3], (TOKENS, FF), 1.0, 6.0, ((0, 8), (1, 32)))
    w_gate = gaussian(seeds[4], (D, FF), D ** -0.5, 0.0625, ((0, 8), (1, 32)))
    w_up = gaussian(seeds[5], (D, FF), D ** -0.5, 0.0625, ((0, 8), (1, 32)))
    w_down = gaussian(seeds[6], (FF, D), FF ** -0.5, 0.03125, ((0, 32), (1, 8)))
    return dict(block_input=block_input, output_grad=output_grad, gate_pre=gate_pre, up_pre=up_pre, w_gate=w_gate, w_up=w_up, w_down=w_down)


def swiglu_grad(upstream, gate_pre, up_pre):
    gate_vals = gate_pre.astype(jnp.float32)
    up_vals = up_pre.astype(jnp.float32)
    sigmoid_gate = jax.nn.sigmoid(gate_vals)
    silu_value = gate_vals * sigmoid_gate
    activated = (silu_value * up_vals).astype(jnp.bfloat16)
    up_delta = (upstream * silu_value).astype(jnp.bfloat16)
    gate_delta = (upstream * up_vals * sigmoid_gate * (1.0 + gate_vals * (1.0 - sigmoid_gate))).astype(jnp.bfloat16)
    return (activated, gate_delta, up_delta)

def contract_rows(left, right):
    return lax.dot_general(left, right, (((0,), (0,)), ((), ())), preferred_element_type=jnp.float32)

def contract_cols(left, right):
    return lax.dot_general(left, right, (((1,), (1,)), ((), ())), preferred_element_type=jnp.float32)

def reference(block_input, output_grad, gate_pre, up_pre, w_gate, w_up, w_down):
    block_width = D // N_ROW
    upstream = jnp.zeros((TOKENS, FF), jnp.float32)
    for feature_block in range(N_ROW):
        low_edge = feature_block * block_width
        high_edge = low_edge + block_width
        partial_term = contract_cols(output_grad[:, low_edge:high_edge], w_down[:, low_edge:high_edge])
        rounded = lax.optimization_barrier(partial_term.astype(jnp.bfloat16))
        upstream = upstream + rounded.astype(jnp.float32)
    activated, gate_delta, up_delta = swiglu_grad(upstream, gate_pre, up_pre)
    grad_gate = contract_rows(block_input, gate_delta).astype(jnp.bfloat16)
    grad_up = contract_rows(block_input, up_delta).astype(jnp.bfloat16)
    grad_down = contract_rows(activated, output_grad).astype(jnp.bfloat16)
    grad_input = (contract_cols(gate_delta, w_gate) + contract_cols(up_delta, w_up)).astype(jnp.bfloat16)
    return (grad_input, grad_gate, grad_up, grad_down)
```

```python
import functools

import jax
import jax.numpy as jnp
from jax import lax
from jax.experimental import pallas as pl
from jax.experimental.pallas import tpu as pltpu
from jax.sharding import PartitionSpec as P

MESH = pl.DeviceIdType.MESH
BF, F32 = jnp.bfloat16, jnp.float32
NZ, NCHIP = 8, 16
TB = 128
DB = 1024
FB = 896
PR = 32


def nt(a, b):
    return lax.dot_general(a, b, (((1,), (1,)), ((), ())), preferred_element_type=F32)


def nn(a, b):
    return lax.dot_general(a, b, (((1,), (0,)), ((), ())), preferred_element_type=F32)


def kernel(
    x_h, og_h, g_h, u_h, wg_h, wu_h, wd_h,
    gi_h, gg_h, gu_h, gdn_h,
    og, xa, xt, gv, uv, wg, wu, wd, actt, dl, terms, rs_out, rs_in, acc, stage, gdn, own, cs, cr, sx, rr, gi,
    loc, act_s, act_r, og_s, og_r, ogc_s, ogc_r, x_s, x_r, xc_s, xc_r, rs_s, rs_r, ag_s, ag_r, cs_s, cs_r, rr_s, rr_r, outs,
):
    z, col = lax.axis_index("row"), lax.axis_index("col")
    chip, core = col // 2, lax.rem(col, 2)
    sib = (z, col + 1 - 2 * core)

    def zdev(d):
        return (lax.rem(z + (1 if d == 0 else NZ - 1), NZ), col)

    def zrel(n):
        return lax.rem(z + (n % NZ), NZ)

    def chip_at(j):
        return lax.rem(chip + j + NCHIP, NCHIP)

    def chip_dev(j):
        return (z, 2 * chip_at(j) + core)

    def remote(src, dst, ss, rs, dev):
        return pltpu.make_async_remote_copy(
            src_ref=src, dst_ref=dst, send_sem=ss, recv_sem=rs, device_id=dev, device_id_type=MESH
        )

    mine = pl.ds(pl.multiple_of(col * PR, PR), PR)
    locals_ = [
        pltpu.make_async_copy(og_h, og.at[mine], loc.at[0]),
        pltpu.make_async_copy(g_h, gv, loc.at[1]),
        pltpu.make_async_copy(u_h, uv, loc.at[2]),
        pltpu.make_async_copy(x_h, xa.at[mine], loc.at[3]),
        pltpu.make_async_copy(wd_h, wd, loc.at[4]),
        pltpu.make_async_copy(wg_h, wg, loc.at[5]),
        pltpu.make_async_copy(wu_h, wu, loc.at[6]),
    ]
    for c in locals_:
        c.start()

    bar = pltpu.get_barrier_semaphore()
    for d in (0, 1):
        pl.semaphore_signal(bar, inc=1, device_id=zdev(d), device_id_type=MESH)
    pl.semaphore_signal(bar, inc=1, device_id=sib, device_id_type=MESH)

    def greet(j, _):
        pl.semaphore_signal(bar, inc=1, device_id=chip_dev(j), device_id_type=MESH)
        return 0

    lax.fori_loop(1, NCHIP, greet, 0)
    pl.semaphore_wait(bar, NCHIP + 2)

    def piece(buf, j):
        return buf.at[pl.ds(pl.multiple_of((2 * chip_at(j) + core) * PR, PR), PR)]

    def spread(buf, j, ss, rs):
        return remote(buf.at[mine], buf.at[mine], ss.at[j], rs.at[j], chip_dev(j))

    def landed(buf, j, ss, rs):
        p = piece(buf, NCHIP - j)
        return remote(p, p, ss.at[j], rs.at[j], chip_dev(j))

    def share(buf, j, ss, rs):
        p = piece(buf, NCHIP - j)
        return remote(p, p, ss.at[j], rs.at[j], sib)

    def shared(buf, j, ss, rs):
        p = buf.at[pl.ds(pl.multiple_of((2 * chip_at(NCHIP - j) + 1 - core) * PR, PR), PR)]
        return remote(p, p, ss.at[j], rs.at[j], sib)

    def send_own(buf, s, r, cs_, cr_):
        def body(j, _):
            spread(buf, j, s, r).start()
            return 0

        lax.fori_loop(1, NCHIP, body, 0)
        share(buf, 0, cs_, cr_).start()

    def pass_on(lo, hi, buf, s, r, cs_, cr_):
        def body(j, _):
            landed(buf, j, s, r).wait_recv()
            share(buf, j, cs_, cr_).start()
            return 0

        lax.fori_loop(lo, hi, body, 0)

    def wait_shared(buf, cs_, cr_):
        def body(j, _):
            shared(buf, j, cs_, cr_).wait_recv()
            return 0

        lax.fori_loop(0, NCHIP, body, 0)

    ogx, xx = (og, og_s, og_r, ogc_s, ogc_r), (xa, x_s, x_r, xc_s, xc_r)

    locals_[0].wait()
    send_own(*ogx)

    def hops(d, h):
        return 4 if d == h else 3

    HB = FB // 2

    def act_part(n, h):
        return actt.at[zrel(n), pl.ds(h * HB, HB)]

    def act_send(s):
        for h_ in (0, 1):
            for d in (0, 1):
                h = h_ ^ d
                if s <= hops(d, h):
                    p = act_part((1 - s) if d == 0 else (s - 1), h)
                    remote(p, p, act_s.at[d, s - 1, h], act_r.at[d, s - 1, h], zdev(d)).start()

    def act_take(s):
        for h_ in (0, 1):
            for d in (0, 1):
                h = h_ ^ d
                if s <= hops(d, h):
                    p = act_part(-s if d == 0 else s, h)
                    remote(p, p, act_s.at[d, s - 1, h], act_r.at[d, s - 1, h], zdev(d)).wait_recv()
                    if s + 1 <= hops(d, h):
                        remote(p, p, act_s.at[d, s, h], act_r.at[d, s, h], zdev(d)).start()

    locals_[1].wait()
    locals_[2].wait()
    for q in range(FB // 128):
        cols = pl.ds(q * 128, 128)
        g = gv[:, cols].astype(F32)
        a = (g * jax.nn.sigmoid(g) * uv[:, cols].astype(F32)).astype(BF)
        actt[z, cols, :] = a.astype(F32).T.astype(BF)
    act_send(1)

    pass_on(1, 8, *ogx)
    act_take(1)
    pass_on(8, NCHIP, *ogx)
    wait_shared(og, ogc_s, ogc_r)
    locals_[3].wait()
    send_own(*xx)

    def rows(b):
        return pl.ds(pl.multiple_of(b * TB, TB), TB)

    def make_terms(rels):
        a = jnp.concatenate([og[rows(zrel(r)), :] for r in rels], axis=0) if len(rels) > 1 else og[rows(zrel(rels[0])), :]

        def body(i, _):
            lanes = pl.ds(pl.multiple_of(i * 128, 128), 128)
            t = nt(a, wd[lanes, :])
            for n, r in enumerate(rels):
                terms[r, :, lanes] = t[n * TB : (n + 1) * TB].astype(BF).astype(F32)
            return 0

        lax.fori_loop(0, FB // 128, body, 0)

    def half(h):
        return pl.ds(h * (TB // 2), TB // 2)

    def rs_copy(d, s, h):
        return remote(
            rs_out.at[d, s - 1, half(h)], rs_in.at[d, s - 1, half(h)],
            rs_s.at[d, s - 1, h], rs_r.at[d, s - 1, h], zdev(d),
        )

    def rs_step(s, fresh):
        for h_ in (0, 1):
            for d in (0, 1):
                h = h_ ^ d
                first = 1 if h == d else 2
                if s < first or (s == first) != fresh:
                    continue
                t = terms[5 - s if d == 0 else 3 + s, half(h), :]
                if not fresh:
                    rs_copy(d, s - 1, h).wait_recv()
                    t = t + rs_in[d, s - 2, half(h), :].astype(F32)
                rs_out[d, s - 1, half(h), :] = t.astype(BF)
                rs_copy(d, s, h).start()

    locals_[4].wait()
    make_terms([4])
    rs_step(1, True)
    make_terms([3, 5])
    rs_step(2, True)
    act_take(2)
    rs_step(2, False)
    make_terms([2, 6])
    act_take(3)
    rs_step(3, False)
    make_terms([1, 7])
    make_terms([0])
    pass_on(1, 8, *xx)
    rs_step(4, False)
    act_take(4)
    pass_on(8, NCHIP, *xx)

    for d in (0, 1):
        for h in (0, 1):
            rs_copy(d, 4, h).wait_recv()
    for q in range(FB // 128):
        cols = pl.ds(q * 128, 128)
        g, u = gv[:, cols].astype(F32), uv[:, cols].astype(F32)
        up = terms[0, :, cols] + rs_in[0, 3, :, cols].astype(F32) + rs_in[1, 3, :, cols].astype(F32)
        s = jax.nn.sigmoid(g)
        dl[z, 0, :, cols] = (up * u * s * (1.0 + g * (1.0 - s))).astype(BF)
        dl[z, 1, :, cols] = (up * (g * s)).astype(BF)

    def ag_copy(d, s, a):
        p = dl.at[zrel((1 - s) if d == 0 else (s - 1)), a]
        return remote(p, p, ag_s.at[d, s - 1, a], ag_r.at[d, s - 1, a], zdev(d))

    def ag_take(s):
        for a_ in (0, 1):
            for d in (0, 1):
                a = a_ ^ d
                if s <= hops(d, a):
                    p = dl.at[zrel(-s if d == 0 else s), a]
                    remote(p, p, ag_s.at[d, s - 1, a], ag_r.at[d, s - 1, a], zdev(d)).wait_recv()
                    if s + 1 <= hops(d, a):
                        ag_copy(d, s + 1, a).start()

    for a_ in (0, 1):
        for d in (0, 1):
            ag_copy(d, 1, a_ ^ d).start()

    def down(i, _):
        r = pl.ds(pl.multiple_of(i * 128, 128), 128)
        a = jnp.concatenate([actt[b, r, :] for b in range(NZ)], axis=1)
        gdn[r, :] = nn(a, og[...]).astype(BF)
        return 0

    lax.fori_loop(0, FB // 128, down, 0)
    out_down = pltpu.make_async_copy(gdn, gdn_h, outs.at[0])
    out_down.start()

    wait_shared(xa, xc_s, xc_r)

    def flip(b, _):
        for q in range(DB // 128):
            v = xa[rows(b), pl.ds(q * 128, 128)].astype(F32)
            xt[b, pl.ds(q * 128, 128), :] = v.T.astype(BF)
        return 0

    lax.fori_loop(0, NZ, flip, 0)
    locals_[5].wait()
    locals_[6].wait()

    def grads(blocks, first, last):
        def cat(vals, axis):
            return vals[0] if len(vals) == 1 else jnp.concatenate(vals, axis=axis)

        def body(i, _):
            r = pl.ds(pl.multiple_of(i * 256, 256), 256)
            xb = cat([xt[b, r, :] for b in blocks], 1)
            for a in (0, 1):
                t = nn(xb, cat([dl[b, a] for b in blocks], 0))
                if not first:
                    t = t + acc[a, r, :]
                if last:
                    stage[a, r, :] = t.astype(BF)
                else:
                    acc[a, r, :] = t
            return 0

        lax.fori_loop(0, DB // 256, body, 0)

    def core_copy(c):
        return remote(cs.at[c], cr.at[c], cs_s.at[c], cs_r.at[c], sib)

    def inputs(blocks):
        gdb = jnp.concatenate([dl[b, 0] for b in blocks], axis=0) if len(blocks) > 1 else dl[blocks[0], 0]
        udb = jnp.concatenate([dl[b, 1] for b in blocks], axis=0) if len(blocks) > 1 else dl[blocks[0], 1]

        def body(i, _):
            n = pl.ds(pl.multiple_of(i * 256, 256), 256)
            t = nt(gdb, wg[n, :]) + nt(udb, wu[n, :])
            for m, b in enumerate(blocks):
                for e in (0, 1):
                    base = m * TB + e * 2 * PR
                    lo, hi = t[base : base + PR], t[base + PR : base + 2 * PR]
                    own[2 * b + e, :, n] = jnp.where(core == 0, lo, hi)
                    cs[2 * b + e, :, n] = jnp.where(core == 0, hi, lo).astype(BF)
            return 0

        lax.fori_loop(0, DB // 256, body, 0)
        for b in blocks:
            for e in (0, 1):
                core_copy(2 * b + e).start()

    def reduce_copy(c):
        j = lax.rem(c - chip + NCHIP, NCHIP)
        return remote(sx.at[c], rr.at[j], rr_s.at[j], rr_r.at[j], (z, 2 * c + core))

    def push(blocks):
        for b in blocks:
            for e in (0, 1):
                c = 2 * b + e
                core_copy(c).wait_recv()
                t = own[c] + cr[c].astype(F32)
                own[c] = t
                sx[c] = t.astype(BF)

                @pl.when(c != chip)
                def _():
                    reduce_copy(c).start()

    pending = [z]
    inputs(pending)
    grads(pending, True, False)
    for s in (1, 2, 3):
        ag_take(s)
        push(pending)
        pending = [zrel(-s), zrel(s)]
        inputs(pending)
        grads(pending, False, False)
    push(pending)
    ag_take(4)
    pending = [zrel(4)]
    inputs(pending)
    push(pending)
    grads(pending, False, True)
    out_gate = pltpu.make_async_copy(stage.at[0], gg_h, outs.at[1])
    out_up = pltpu.make_async_copy(stage.at[1], gu_h, outs.at[2])
    out_gate.start()
    out_up.start()

    def arrive(j, _):
        remote(sx.at[0], rr.at[j], rr_s.at[j], rr_r.at[j], sib).wait_recv()
        return 0

    lax.fori_loop(1, NCHIP, arrive, 0)
    total = own[chip]
    for j in range(1, NCHIP):
        total = total + rr[j].astype(F32)
    gi[...] = total.astype(BF)
    out_gi = pltpu.make_async_copy(gi, gi_h, outs.at[3])
    out_gi.start()

    def gone(j, _):
        spread(og, j, og_s, og_r).wait_send()
        spread(xa, j, x_s, x_r).wait_send()
        remote(sx.at[0], rr.at[j], rr_s.at[j], rr_r.at[j], sib).wait_send()
        return 0

    lax.fori_loop(1, NCHIP, gone, 0)

    def gone_core(j, _):
        share(og, j, ogc_s, ogc_r).wait_send()
        share(xa, j, xc_s, xc_r).wait_send()
        core_copy(j).wait_send()
        return 0

    lax.fori_loop(0, NCHIP, gone_core, 0)
    for d in (0, 1):
        for h in (0, 1):
            for s in range(1, 5):
                if s <= hops(d, h):
                    p = act_part(0, h)
                    remote(p, p, act_s.at[d, s - 1, h], act_r.at[d, s - 1, h], zdev(d)).wait_send()
                    ag_copy(d, s, h).wait_send()
                if s >= (1 if h == d else 2):
                    rs_copy(d, s, h).wait_send()
    out_down.wait()
    out_gate.wait()
    out_up.wait()
    out_gi.wait()


def on_device(block_input, output_grad, gate_pre, up_pre, w_gate, w_up, w_down):
    dma = pltpu.SemaphoreType.DMA
    any_ = pl.BlockSpec(memory_space=pl.ANY)
    ring = [dma((2, 4, 2))] * 2
    plane = [dma((NCHIP,))] * 2
    return pl.pallas_call(
        kernel,
        out_shape=(
            jax.ShapeDtypeStruct((PR, DB), BF),
            jax.ShapeDtypeStruct((DB, FB), BF),
            jax.ShapeDtypeStruct((DB, FB), BF),
            jax.ShapeDtypeStruct((FB, DB), BF),
        ),
        in_specs=[any_] * 7,
        out_specs=(any_,) * 4,
        scratch_shapes=[
            pltpu.VMEM((1024, DB), BF),
            pltpu.VMEM((1024, DB), BF),
            pltpu.VMEM((NZ, DB, TB), BF),
            pltpu.VMEM((TB, FB), BF),
            pltpu.VMEM((TB, FB), BF),
            pltpu.VMEM((DB, FB), BF),
            pltpu.VMEM((DB, FB), BF),
            pltpu.VMEM((FB, DB), BF),
            pltpu.VMEM((NZ, FB, TB), BF),
            pltpu.VMEM((NZ, 2, TB, FB), BF),
            pltpu.VMEM((NZ, TB, FB), F32),
            pltpu.VMEM((2, 4, TB, FB), BF),
            pltpu.VMEM((2, 4, TB, FB), BF),
            pltpu.VMEM((2, DB, FB), F32),
            pltpu.VMEM((2, DB, FB), BF),
            pltpu.VMEM((FB, DB), BF),
            pltpu.VMEM((NCHIP, PR, DB), F32),
            pltpu.VMEM((NCHIP, PR, DB), BF),
            pltpu.VMEM((NCHIP, PR, DB), BF),
            pltpu.VMEM((NCHIP, PR, DB), BF),
            pltpu.VMEM((NCHIP, PR, DB), BF),
            pltpu.VMEM((PR, DB), BF),
            dma((7,)),
            *ring,
            *plane, *plane,
            *plane, *plane,
            *ring,
            *ring,
            *plane,
            *plane,
            dma((4,)),
        ],
        compiler_params=pltpu.CompilerParams(
            collective_id=0, has_side_effects=True, vmem_limit_bytes=56 * 2**20
        ),
        name="ffn_grad",
    )(block_input, output_grad, gate_pre, up_pre, w_gate, w_up, w_down)


def solution(mesh):
    return jax.shard_map(
        on_device,
        mesh=mesh,
        in_specs=(
            P("col", "row"),
            P("col", "row"),
            P("row", "col"),
            P("row", "col"),
            P("row", "col"),
            P("row", "col"),
            P("col", "row"),
        ),
        out_specs=(P("col", "row"), P("row", "col"), P("row", "col"), P("col", "row")),
        check_vma=False,
    )
```

```python
import functools

import jax
import jax.numpy as jnp
from jax import lax
from jax.experimental import pallas as pl
from jax.experimental.pallas import tpu as pltpu
from jax.sharding import PartitionSpec as P

MESH = pl.DeviceIdType.MESH
BF, F32 = jnp.bfloat16, jnp.float32
NZ, NCHIP = 8, 16
TB = 128
HT = 64
DB = 1024
FB = 896
PR = 32


def nt(a, b):
    return lax.dot_general(a, b, (((1,), (1,)), ((), ())), preferred_element_type=F32)


def nn(a, b):
    return lax.dot_general(a, b, (((1,), (0,)), ((), ())), preferred_element_type=F32)


def kernel(
    x_h, og_h, g_h, u_h, wg_h, wu_h, wd_h,
    gi, stage_g, stage_u, gdn,
    og, xa, xt, gu, gl, wg, wu, wd, act, up, dl, terms, rs_out, rs_in, acc, own, cs, cr, s1, r1, s2, rr,
    loc, ring_s, ring_r, og_s, og_r, ogc_s, ogc_r, x_s, x_r, xc_s, xc_r, rs_s, rs_r, cs_s, cs_r, p1_s, p1_r, rr_s, rr_r,
):
    z, col = lax.axis_index("row"), lax.axis_index("col")
    chip, core = col // 2, lax.rem(col, 2)
    cx = chip // 4
    sib = (z, col + 1 - 2 * core)

    def zdev(d):
        return (lax.rem(z + (1 if d == 0 else NZ - 1), NZ), col)

    def zrel(n):
        return lax.rem(z + (n % NZ), NZ)

    def chip_at(j):
        return lax.rem(chip + j + NCHIP, NCHIP)

    def chip_dev(j):
        return (z, 2 * chip_at(j) + core)

    def remote(src, dst, ss, rs, dev):
        return pltpu.make_async_remote_copy(
            src_ref=src, dst_ref=dst, send_sem=ss, recv_sem=rs, device_id=dev, device_id_type=MESH
        )

    mine = pl.ds(pl.multiple_of(col * PR, PR), PR)
    locals_ = [
        pltpu.make_async_copy(g_h.at[pl.ds(0, HT)], gu.at[z, 0], loc.at[0]),
        pltpu.make_async_copy(u_h.at[pl.ds(0, HT)], gu.at[z, 1], loc.at[1]),
        pltpu.make_async_copy(og_h, og.at[mine], loc.at[2]),
        pltpu.make_async_copy(g_h.at[pl.ds(HT, HT)], gl.at[0], loc.at[3]),
        pltpu.make_async_copy(u_h.at[pl.ds(HT, HT)], gl.at[1], loc.at[4]),
        pltpu.make_async_copy(x_h, xa.at[mine], loc.at[5]),
        pltpu.make_async_copy(wd_h, wd, loc.at[6]),
        pltpu.make_async_copy(wg_h, wg, loc.at[7]),
        pltpu.make_async_copy(wu_h, wu, loc.at[8]),
    ]
    for c in locals_:
        c.start()

    bar = pltpu.get_barrier_semaphore()
    for d in (0, 1):
        pl.semaphore_signal(bar, inc=1, device_id=zdev(d), device_id_type=MESH)
    pl.semaphore_signal(bar, inc=1, device_id=sib, device_id_type=MESH)

    def greet(j, _):
        pl.semaphore_signal(bar, inc=1, device_id=chip_dev(j), device_id_type=MESH)
        return 0

    lax.fori_loop(1, NCHIP, greet, 0)
    pl.semaphore_wait(bar, NCHIP + 2)

    def piece(buf, j):
        return buf.at[pl.ds(pl.multiple_of((2 * chip_at(j) + core) * PR, PR), PR)]

    def spread(buf, j, ss, rs):
        return remote(buf.at[mine], buf.at[mine], ss.at[j], rs.at[j], chip_dev(j))

    def landed(buf, j, ss, rs):
        p = piece(buf, NCHIP - j)
        return remote(p, p, ss.at[j], rs.at[j], chip_dev(j))

    def share(buf, j, ss, rs):
        p = piece(buf, NCHIP - j)
        return remote(p, p, ss.at[j], rs.at[j], sib)

    def shared(buf, j, ss, rs):
        p = buf.at[pl.ds(pl.multiple_of((2 * chip_at(NCHIP - j) + 1 - core) * PR, PR), PR)]
        return remote(p, p, ss.at[j], rs.at[j], sib)

    def send_own(buf, s, r, cs_, cr_):
        def body(j, _):
            spread(buf, j, s, r).start()
            return 0

        lax.fori_loop(1, NCHIP, body, 0)
        share(buf, 0, cs_, cr_).start()

    def pass_on(lo, hi, buf, s, r, cs_, cr_):
        def body(j, _):
            landed(buf, j, s, r).wait_recv()
            share(buf, j, cs_, cr_).start()
            return 0

        lax.fori_loop(lo, hi, body, 0)

    def wait_shared(buf, cs_, cr_):
        def body(j, _):
            shared(buf, j, cs_, cr_).wait_recv()
            return 0

        lax.fori_loop(0, NCHIP, body, 0)

    ogx, xx = (og, og_s, og_r, ogc_s, ogc_r), (xa, x_s, x_r, xc_s, xc_r)

    G, U, UP, GD, UD, ACT = range(6)
    low, high = pl.ds(0, HT), pl.ds(HT, HT)

    def ring_ref(i, n):
        b = zrel(n)
        return (
            lambda: gu.at[b, 0],
            lambda: gu.at[b, 1],
            lambda: up.at[b],
            lambda: dl.at[b, 0, high],
            lambda: dl.at[b, 1, high],
            lambda: act.at[b, high],
        )[i]()

    LONG = (0, 1, 1, 0, 1, 0)

    def hops(d, i):
        return 4 if LONG[i] == d else 3

    def ring_copy(i, d, s, n):
        p = ring_ref(i, n)
        return remote(p, p, ring_s.at[i, d, s - 1], ring_r.at[i, d, s - 1], zdev(d))

    def ring_send(i):
        for d in (LONG[i], 1 - LONG[i]):
            ring_copy(i, d, 1, 0).start()

    def ring_take(i, s):
        for d in (LONG[i], 1 - LONG[i]):
            if s <= hops(d, i):
                n = -s if d == 0 else s
                ring_copy(i, d, s, n).wait_recv()
                if s + 1 <= hops(d, i):
                    ring_copy(i, d, s + 1, n).start()

    locals_[0].wait()
    ring_send(G)
    locals_[1].wait()
    ring_send(U)
    locals_[2].wait()
    send_own(*ogx)

    def silu_parts(g, u):
        s = jax.nn.sigmoid(g)
        return g * s, u * s * (1.0 + g * (1.0 - s))

    def tiles(body):
        def step(q, _):
            body(pl.ds(pl.multiple_of(q * 128, 128), 128))
            return 0

        lax.fori_loop(0, FB // 128, step, 0)

    locals_[3].wait()
    locals_[4].wait()

    def own_act(cols):
        g, u = gl[0, :, cols].astype(F32), gl[1, :, cols].astype(F32)
        act[z, high, cols] = (g * jax.nn.sigmoid(g) * u).astype(BF)

    tiles(own_act)

    ring_send(ACT)
    ring_take(G, 1)
    ring_take(U, 1)
    pass_on(1, 4, *ogx)
    ring_take(ACT, 1)
    pass_on(4, 10, *ogx)
    ring_take(G, 2)
    pass_on(10, NCHIP, *ogx)
    ring_take(U, 2)
    wait_shared(og, ogc_s, ogc_r)

    def rows(b):
        return pl.ds(pl.multiple_of(b * TB, TB), TB)

    def make_terms(rels):
        a = jnp.concatenate([og[rows(zrel(r)), :] for r in rels], axis=0) if len(rels) > 1 else og[rows(zrel(rels[0])), :]

        def tile(lanes):
            t = nt(a, wd[lanes, :])
            for n, r in enumerate(rels):
                terms[r, :, lanes] = t[n * TB : (n + 1) * TB].astype(BF).astype(F32)

        def body(i, _):
            tile(pl.ds(pl.multiple_of(i * 256, 256), 256))
            return 0

        lax.fori_loop(0, 3, body, 0)
        tile(pl.ds(768, 128))

    QT = TB // 4

    def rs_copy(d, s, q):
        r = pl.ds(q * QT, QT)
        return remote(
            rs_out.at[d, s - 1, r], rs_in.at[d, s - 1, r], rs_s.at[d, s - 1, q], rs_r.at[d, s - 1, q], zdev(d)
        )

    def rs_step(s, fresh):
        for o in (2, 3, 0, 1):
            for d in (0, 1):
                q = o ^ (2 * d)
                first = 1 if o < 2 else 2
                if s < first or (s == first) != fresh:
                    continue
                r = pl.ds(q * QT, QT)
                t = terms[5 - s if d == 0 else 3 + s, r, :]
                if not fresh:
                    rs_copy(d, s - 1, q).wait_recv()
                    t = t + rs_in[d, s - 2, r, :].astype(F32)
                rs_out[d, s - 1, r, :] = t.astype(BF)
                rs_copy(d, s, q).start()

    def all_act(lo, hi):
        def block(b, _):
            def body(cols):
                g, u = gu[b, 0, :, cols].astype(F32), gu[b, 1, :, cols].astype(F32)
                act[b, low, cols] = (g * jax.nn.sigmoid(g) * u).astype(BF)

            tiles(body)
            return 0

        lax.fori_loop(lo, hi, block, 0)

    def down(lo, hi, width):
        def body(i, _):
            cols = pl.ds(pl.multiple_of(i * width, width), width)
            a = jnp.concatenate([act[b, :, cols] for b in range(NZ)], axis=0)
            gdn[cols, :] = nn(a.astype(F32).T.astype(BF), og[...]).astype(BF)
            return 0

        lax.fori_loop(lo, hi, body, 0)

    def flip(b, _):
        for q in range(DB // 128):
            v = xa[rows(b), pl.ds(q * 128, 128)].astype(F32)
            xt[b, pl.ds(q * 128, 128), :] = v.T.astype(BF)
        return 0

    locals_[6].wait()
    make_terms([4])
    rs_step(1, True)
    make_terms([3, 5, 2, 6])
    rs_step(2, True)
    ring_take(G, 3)
    locals_[5].wait()
    send_own(*xx)
    rs_step(2, False)
    ring_take(U, 3)
    make_terms([1, 7, 0])
    rs_step(3, False)
    ring_take(G, 4)
    ring_take(U, 4)
    rs_step(4, False)
    ring_take(ACT, 2)
    pass_on(1, NCHIP, *xx)
    all_act(0, 8)

    for d in (0, 1):
        for q in (0, 1):
            rs_copy(d, 4, q).wait_recv()

    def own_up(cols):
        t = terms[0, low, cols] + rs_in[0, 3, low, cols].astype(F32) + rs_in[1, 3, low, cols].astype(F32)
        up[z, :, cols] = t.astype(BF)

    tiles(own_up)
    ring_send(UP)
    for d in (0, 1):
        for q in (2, 3):
            rs_copy(d, 4, q).wait_recv()

    def own_deltas(cols):
        t = terms[0, high, cols] + rs_in[0, 3, high, cols].astype(F32) + rs_in[1, 3, high, cols].astype(F32)
        su, sg = silu_parts(gl[0, :, cols].astype(F32), gl[1, :, cols].astype(F32))
        dl[z, 0, high, cols] = (t * sg).astype(BF)
        dl[z, 1, high, cols] = (t * su).astype(BF)

    tiles(own_deltas)
    ring_send(GD)
    ring_send(UD)

    def deltas(blocks):
        for b in blocks:

            def body(cols, b=b):
                su, sg = silu_parts(gu[b, 0, :, cols].astype(F32), gu[b, 1, :, cols].astype(F32))
                t = up[b, :, cols].astype(F32)
                dl[b, 0, low, cols] = (t * sg).astype(BF)
                dl[b, 1, low, cols] = (t * su).astype(BF)

            tiles(body)

    wait_shared(xa, xc_s, xc_r)
    lax.fori_loop(0, NZ, flip, 0)
    locals_[7].wait()
    locals_[8].wait()

    def grads(blocks, first, last):
        def cat(vals, axis):
            return vals[0] if len(vals) == 1 else jnp.concatenate(vals, axis=axis)

        def body(i, _):
            r = pl.ds(pl.multiple_of(i * 512, 512), 512)
            xb = cat([xt[b, r, :] for b in blocks], 1)
            for a in (0, 1):
                t = nn(xb, cat([dl[b, a] for b in blocks], 0))
                if not first:
                    t = t + acc[a, r, :]
                if last:
                    (stage_g, stage_u)[a][r, :] = t.astype(BF)
                else:
                    acc[a, r, :] = t
            return 0

        lax.fori_loop(0, DB // 512, body, 0)

    def core_copy(b):
        return remote(cs.at[b], cr.at[b], cs_s.at[b], cs_r.at[b], sib)

    def x_copy(b, dx):
        return remote(s1.at[b, dx], r1.at[b, dx], p1_s.at[b, dx], p1_r.at[b, dx], chip_dev(4 * dx))

    def inputs(blocks):
        gdb = jnp.concatenate([dl[b, 0] for b in blocks], axis=0) if len(blocks) > 1 else dl[blocks[0], 0]
        udb = jnp.concatenate([dl[b, 1] for b in blocks], axis=0) if len(blocks) > 1 else dl[blocks[0], 1]

        def body(i, _):
            n = pl.ds(pl.multiple_of(i * 256, 256), 256)
            t = nt(gdb, wg[n, :]) + nt(udb, wu[n, :])
            for m, b in enumerate(blocks):
                for e in (0, 1):
                    base = m * TB + e * 2 * PR
                    lo, hi = t[base : base + PR], t[base + PR : base + 2 * PR]
                    own[b, i, pl.ds(e * PR, PR), :] = jnp.where(core == 0, lo, hi)
                    cs[b, i, pl.ds(e * PR, PR), :] = jnp.where(core == 0, hi, lo).astype(BF)
            return 0

        lax.fori_loop(0, DB // 256, body, 0)
        for b in blocks:
            core_copy(b).start()

    def sum_cores(blocks):
        for b in blocks:
            core_copy(b).wait_recv()
            for dx in (1, 2, 3, 0):
                i = lax.rem(cx + dx, 4)
                t = own[b, i] + cr[b, i].astype(F32)
                if dx == 0:
                    own[b, i] = t
                else:
                    s1[b, dx] = t.astype(BF)
                    x_copy(b, dx).start()

    def reduce_copy(b, e, j):
        return remote(
            s2.at[b, pl.ds(e * PR, PR)], rr.at[j], rr_s.at[j], rr_r.at[j], (z, 2 * (2 * b + e) + core)
        )

    def sum_x(blocks):
        for b in blocks:
            t = own[b, cx]
            for dx in (1, 2, 3):
                x_copy(b, dx).wait_recv()
                t = t + r1[b, dx].astype(F32)
            own[b, cx] = t
            s2[b] = t.astype(BF)
            for e in (0, 1):
                c = 2 * b + e

                @pl.when(c != chip)
                def _(b=b, e=e, c=c):
                    reduce_copy(b, e, lax.rem(c - chip + NCHIP, NCHIP)).start()

    def step_blocks(s):
        return [z] if s == 0 else [zrel(4)] if s == 4 else [zrel(-s), zrel(s)]

    deltas(step_blocks(0))
    inputs(step_blocks(0))
    ring_take(UP, 1)
    grads(step_blocks(0), True, False)
    ring_take(GD, 1)
    sum_cores(step_blocks(0))
    ring_take(UD, 1)
    for s in (1, 2, 3):
        now, before = step_blocks(s), step_blocks(s - 1)
        deltas(now)
        inputs(now)
        ring_take(UP, s + 1)
        grads(now, False, False)
        ring_take(GD, s + 1)
        sum_x(before)
        sum_cores(now)
        ring_take(UD, s + 1)
        if s == 2:
            ring_take(ACT, 3)
    now = step_blocks(4)
    deltas(now)
    inputs(now)
    sum_x(step_blocks(3))
    sum_cores(now)
    grads(now, False, True)
    sum_x(now)
    ring_take(ACT, 4)
    down(0, 3, 256)
    down(6, 7, 128)

    def arrive(j, _):
        remote(s2.at[0, pl.ds(0, PR)], rr.at[j], rr_s.at[j], rr_r.at[j], sib).wait_recv()
        return 0

    lax.fori_loop(1, NCHIP, arrive, 0)
    rr[0] = own[chip // 2, cx, pl.ds(pl.multiple_of(lax.rem(chip, 2) * PR, PR), PR), :].astype(BF)
    for q in range(4):
        t = jnp.zeros((PR, 256), F32)
        for yy in range(4):
            t = t + rr[lax.rem(chip - (4 * q + yy) + NCHIP, NCHIP)].astype(F32)
        gi[:, q * 256 : (q + 1) * 256] = t.astype(BF)

    def gone(j, _):
        spread(og, j, og_s, og_r).wait_send()
        spread(xa, j, x_s, x_r).wait_send()
        remote(s2.at[0, pl.ds(0, PR)], rr.at[j], rr_s.at[j], rr_r.at[j], sib).wait_send()
        return 0

    lax.fori_loop(1, NCHIP, gone, 0)

    def gone_core(j, _):
        share(og, j, ogc_s, ogc_r).wait_send()
        share(xa, j, xc_s, xc_r).wait_send()
        return 0

    lax.fori_loop(0, NCHIP, gone_core, 0)

    def gone_block(b, _):
        core_copy(b).wait_send()
        for dx in (1, 2, 3):
            x_copy(b, dx).wait_send()
        return 0

    lax.fori_loop(0, NZ, gone_block, 0)
    for d in (0, 1):
        for i in range(6):
            for s in range(1, hops(d, i) + 1):
                ring_copy(i, d, s, 0).wait_send()
        for q in range(4):
            for s in range(1 if q // 2 == d else 2, 5):
                rs_copy(d, s, q).wait_send()


def write_out(*refs):
    sems = refs[8]
    copies = [pltpu.make_async_copy(refs[i], refs[4 + i], sems.at[i]) for i in range(4)]
    for c in copies:
        c.start()
    for c in copies:
        c.wait()


def on_device(block_input, output_grad, gate_pre, up_pre, w_gate, w_up, w_down):
    dma = pltpu.SemaphoreType.DMA
    any_ = pl.BlockSpec(memory_space=pl.ANY)
    plane = [dma((NCHIP,))] * 2
    shapes = ((PR, DB), (DB, FB), (DB, FB), (FB, DB))
    vmem = pl.BlockSpec(memory_space=pltpu.VMEM)
    held = pl.pallas_call(
        kernel,
        out_shape=tuple(pltpu.VMEM(s, BF) for s in shapes),
        in_specs=[any_] * 7,
        out_specs=(vmem,) * 4,
        scratch_shapes=[
            pltpu.VMEM((1024, DB), BF),
            pltpu.VMEM((1024, DB), BF),
            pltpu.VMEM((NZ, DB, TB), BF),
            pltpu.VMEM((NZ, 2, HT, FB), BF),
            pltpu.VMEM((2, HT, FB), BF),
            pltpu.VMEM((DB, FB), BF),
            pltpu.VMEM((DB, FB), BF),
            pltpu.VMEM((FB, DB), BF),
            pltpu.VMEM((NZ, TB, FB), BF),
            pltpu.VMEM((NZ, HT, FB), BF),
            pltpu.VMEM((NZ, 2, TB, FB), BF),
            pltpu.VMEM((NZ, TB, FB), F32),
            pltpu.VMEM((2, 4, TB, FB), BF),
            pltpu.VMEM((2, 4, TB, FB), BF),
            pltpu.VMEM((2, DB, FB), F32),
            pltpu.VMEM((NZ, 4, 2 * PR, 256), F32),
            pltpu.VMEM((NZ, 4, 2 * PR, 256), BF),
            pltpu.VMEM((NZ, 4, 2 * PR, 256), BF),
            pltpu.VMEM((NZ, 4, 2 * PR, 256), BF),
            pltpu.VMEM((NZ, 4, 2 * PR, 256), BF),
            pltpu.VMEM((NZ, 2 * PR, 256), BF),
            pltpu.VMEM((NCHIP, PR, 256), BF),
            dma((9,)),
            *[dma((6, 2, 4))] * 2,
            *plane, *plane,
            *plane, *plane,
            *[dma((2, 4, 4))] * 2,
            *[dma((NZ,))] * 2,
            *[dma((NZ, 4))] * 2,
            *plane,
        ],
        compiler_params=pltpu.CompilerParams(
            collective_id=0, has_side_effects=True, vmem_limit_bytes=56 * 2**20
        ),
        name="ffn_grad",
    )(block_input, output_grad, gate_pre, up_pre, w_gate, w_up, w_down)
    return pl.pallas_call(
        write_out,
        out_shape=tuple(jax.ShapeDtypeStruct(s, BF) for s in shapes),
        in_specs=[vmem] * 4,
        out_specs=(any_,) * 4,
        scratch_shapes=[dma((4,))],
        compiler_params=pltpu.CompilerParams(vmem_limit_bytes=2**20),
        name="write_out",
    )(*held)


def solution(mesh):
    return jax.shard_map(
        on_device,
        mesh=mesh,
        in_specs=(
            P("col", "row"),
            P("col", "row"),
            P("row", "col"),
            P("row", "col"),
            P("row", "col"),
            P("row", "col"),
            P("col", "row"),
        ),
        out_specs=(P("col", "row"), P("row", "col"), P("row", "col"), P("col", "row")),
        check_vma=False,
    )
```

```python
import functools

import jax
import jax.numpy as jnp
from jax import lax
from jax.experimental import pallas as pl
from jax.experimental.pallas import tpu as pltpu
from jax.sharding import PartitionSpec as P

MESH = pl.DeviceIdType.MESH
BF, F32 = jnp.bfloat16, jnp.float32
NZ, NCHIP = 8, 16
TB = 128
HT = 64
DB = 1024
FB = 896
PR = 32


def nt(a, b):
    return lax.dot_general(a, b, (((1,), (1,)), ((), ())), preferred_element_type=F32)


def nn(a, b):
    return lax.dot_general(a, b, (((1,), (0,)), ((), ())), preferred_element_type=F32)


def kernel(
    x_h, og_h, g_h, u_h, wg_h, wu_h, wd_h,
    gi, stage_g, stage_u, gdn,
    og, xa, xt, gu, gl, wg, wu, wd, act, up, dl, terms, rs_out, rs_in, acc, own, cs, cr, s1, r1, s2, rr,
    loc, ring_s, ring_r, og_s, og_r, ogc_s, ogc_r, x_s, x_r, xc_s, xc_r, rs_s, rs_r, cs_s, cs_r, p1_s, p1_r, rr_s, rr_r,
):
    z, col = lax.axis_index("row"), lax.axis_index("col")
    chip, core = col // 2, lax.rem(col, 2)
    cx, cy = chip // 4, lax.rem(chip, 4)
    sib = (z, col + 1 - 2 * core)

    def zdev(d):
        return (lax.rem(z + (1 if d == 0 else NZ - 1), NZ), col)

    def zrel(n):
        return lax.rem(z + (n % NZ), NZ)

    def chip_at(j):
        return lax.rem(chip + j + NCHIP, NCHIP)

    def chip_dev(j):
        return (z, 2 * chip_at(j) + core)

    def remote(src, dst, ss, rs, dev):
        return pltpu.make_async_remote_copy(
            src_ref=src, dst_ref=dst, send_sem=ss, recv_sem=rs, device_id=dev, device_id_type=MESH
        )

    mine = pl.ds(pl.multiple_of(col * PR, PR), PR)
    locals_ = [
        pltpu.make_async_copy(g_h.at[pl.ds(0, HT)], gu.at[z, 0], loc.at[0]),
        pltpu.make_async_copy(u_h.at[pl.ds(0, HT)], gu.at[z, 1], loc.at[1]),
        pltpu.make_async_copy(og_h, og.at[mine], loc.at[2]),
        pltpu.make_async_copy(g_h.at[pl.ds(HT, HT)], gl.at[0], loc.at[3]),
        pltpu.make_async_copy(u_h.at[pl.ds(HT, HT)], gl.at[1], loc.at[4]),
        pltpu.make_async_copy(x_h, xa.at[mine], loc.at[5]),
        pltpu.make_async_copy(wd_h, wd, loc.at[6]),
        pltpu.make_async_copy(wg_h, wg, loc.at[7]),
        pltpu.make_async_copy(wu_h, wu, loc.at[8]),
    ]
    for c in locals_:
        c.start()

    bar = pltpu.get_barrier_semaphore()
    for d in (0, 1):
        pl.semaphore_signal(bar, inc=1, device_id=zdev(d), device_id_type=MESH)
    pl.semaphore_signal(bar, inc=1, device_id=sib, device_id_type=MESH)

    def greet(j, _):
        pl.semaphore_signal(bar, inc=1, device_id=chip_dev(j), device_id_type=MESH)
        return 0

    lax.fori_loop(1, NCHIP, greet, 0)
    pl.semaphore_wait(bar, NCHIP + 2)

    def piece(buf, j):
        return buf.at[pl.ds(pl.multiple_of((2 * chip_at(j) + core) * PR, PR), PR)]

    def spread(buf, j, ss, rs):
        return remote(buf.at[mine], buf.at[mine], ss.at[j], rs.at[j], chip_dev(j))

    def landed(buf, j, ss, rs):
        p = piece(buf, NCHIP - j)
        return remote(p, p, ss.at[j], rs.at[j], chip_dev(j))

    def share(buf, j, ss, rs):
        p = piece(buf, NCHIP - j)
        return remote(p, p, ss.at[j], rs.at[j], sib)

    def shared(buf, j, ss, rs):
        p = buf.at[pl.ds(pl.multiple_of((2 * chip_at(NCHIP - j) + 1 - core) * PR, PR), PR)]
        return remote(p, p, ss.at[j], rs.at[j], sib)

    def send_own(buf, s, r, cs_, cr_):
        def body(j, _):
            spread(buf, j, s, r).start()
            return 0

        lax.fori_loop(1, NCHIP, body, 0)
        share(buf, 0, cs_, cr_).start()

    def pass_on(lo, hi, buf, s, r, cs_, cr_):
        def body(j, _):
            landed(buf, j, s, r).wait_recv()
            share(buf, j, cs_, cr_).start()
            return 0

        lax.fori_loop(lo, hi, body, 0)

    def wait_shared(buf, cs_, cr_):
        def body(j, _):
            shared(buf, j, cs_, cr_).wait_recv()
            return 0

        lax.fori_loop(0, NCHIP, body, 0)

    xx = (xa, x_s, x_r, xc_s, xc_r)

    def chip_xy(dx, dy):
        return lax.rem(cx + dx + 4, 4) * 4 + lax.rem(cy + dy + 4, 4)

    def og_rows(dx, dy, h):
        return og.at[pl.ds(pl.multiple_of((2 * chip_xy(-dx, -dy) + core) * PR + h * 16, 16), 16)]

    def og_copy(h, dx, dy):
        if h == 0:
            p, to = og_rows(dx if dy else 0, 0, 0), (0, dy) if dy else (dx, 0)
        else:
            p, to = og_rows(0, dy if dx else 0, 1), (dx, 0) if dx else (0, dy)
        j = 4 * dx + dy
        return remote(p, p, og_s.at[h, j], og_r.at[h, j], (z, 2 * chip_xy(*to) + core))

    def og_wait(h, dx, dy):
        p, j = og_rows(dx, dy, h), 4 * dx + dy
        remote(p, p, og_s.at[h, j], og_r.at[h, j], sib).wait_recv()

    def og_share(dx, dy, their):
        c = 2 * chip_xy(-dx, -dy) + (1 - core if their else core)
        p, j = og.at[pl.ds(pl.multiple_of(c * PR, PR), PR)], 4 * dx + dy
        return remote(p, p, ogc_s.at[j], ogc_r.at[j], sib)

    FAR = (1, 3, 2)
    OFFSETS = [(dx, dy) for dx in range(4) for dy in range(4)]

    def og_start():
        for n in FAR:
            og_copy(0, n, 0).start()
            og_copy(1, 0, n).start()
        og_share(0, 0, False).start()
        for n in FAR:
            og_copy(0, 0, n).start()
            og_copy(1, n, 0).start()

    def og_turn():
        for n in FAR:
            og_wait(0, n, 0)
            for m in FAR:
                og_copy(0, n, m).start()
            og_wait(1, 0, n)
            for m in FAR:
                og_copy(1, m, n).start()

    def og_finish(offsets):
        for dx, dy in offsets:
            if dy:
                og_wait(0, dx, dy)
            if dx:
                og_wait(1, dx, dy)
            if dx or dy:
                og_share(dx, dy, False).start()


    G, U, UP, GD, UD, ACT = range(6)
    low, high = pl.ds(0, HT), pl.ds(HT, HT)

    def ring_ref(i, n):
        b = zrel(n)
        return (
            lambda: gu.at[b, 0],
            lambda: gu.at[b, 1],
            lambda: up.at[b],
            lambda: dl.at[b, 0, high],
            lambda: dl.at[b, 1, high],
            lambda: act.at[b, high],
        )[i]()

    LONG = (0, 1, 1, 0, 1, 0)

    def hops(d, i):
        return 4 if LONG[i] == d else 3

    def ring_copy(i, d, s, n):
        p = ring_ref(i, n)
        return remote(p, p, ring_s.at[i, d, s - 1], ring_r.at[i, d, s - 1], zdev(d))

    def ring_send(i):
        for d in (LONG[i], 1 - LONG[i]):
            ring_copy(i, d, 1, 0).start()

    def ring_take(i, s):
        for d in (LONG[i], 1 - LONG[i]):
            if s <= hops(d, i):
                n = -s if d == 0 else s
                ring_copy(i, d, s, n).wait_recv()
                if s + 1 <= hops(d, i):
                    ring_copy(i, d, s + 1, n).start()

    locals_[0].wait()
    ring_send(G)
    locals_[1].wait()
    ring_send(U)
    locals_[2].wait()
    og_start()

    def silu_parts(g, u):
        s = jax.nn.sigmoid(g)
        return g * s, u * s * (1.0 + g * (1.0 - s))

    def tiles(body):
        def step(q, _):
            body(pl.ds(pl.multiple_of(q * 128, 128), 128))
            return 0

        lax.fori_loop(0, FB // 128, step, 0)

    locals_[3].wait()
    locals_[4].wait()

    def own_act(cols):
        g, u = gl[0, :, cols].astype(F32), gl[1, :, cols].astype(F32)
        act[z, high, cols] = (g * jax.nn.sigmoid(g) * u).astype(BF)

    tiles(own_act)

    ring_send(ACT)
    og_turn()
    ring_take(G, 1)
    ring_take(U, 1)
    og_finish(OFFSETS[:8])
    ring_take(ACT, 1)
    og_finish(OFFSETS[8:])
    for n in OFFSETS:
        og_share(*n, True).wait_recv()

    def rows(b):
        return pl.ds(pl.multiple_of(b * TB, TB), TB)

    def make_terms(rels):
        a = jnp.concatenate([og[rows(zrel(r)), :] for r in rels], axis=0) if len(rels) > 1 else og[rows(zrel(rels[0])), :]

        def tile(lanes):
            t = nt(a, wd[lanes, :])
            for n, r in enumerate(rels):
                terms[r, :, lanes] = t[n * TB : (n + 1) * TB].astype(BF).astype(F32)

        def body(i, _):
            tile(pl.ds(pl.multiple_of(i * 256, 256), 256))
            return 0

        lax.fori_loop(0, 3, body, 0)
        tile(pl.ds(768, 128))

    QT = TB // 4

    def rs_copy(d, s, q):
        r = pl.ds(q * QT, QT)
        return remote(
            rs_out.at[d, s - 1, r], rs_in.at[d, s - 1, r], rs_s.at[d, s - 1, q], rs_r.at[d, s - 1, q], zdev(d)
        )

    def rs_step(s, fresh):
        for o in (2, 3, 0, 1):
            for d in (0, 1):
                q = o ^ (2 * d)
                first = 1 if o < 2 else 2
                if s < first or (s == first) != fresh:
                    continue
                r = pl.ds(q * QT, QT)
                t = terms[5 - s if d == 0 else 3 + s, r, :]
                if not fresh:
                    rs_copy(d, s - 1, q).wait_recv()
                    t = t + rs_in[d, s - 2, r, :].astype(F32)
                rs_out[d, s - 1, r, :] = t.astype(BF)
                rs_copy(d, s, q).start()

    def all_act(lo, hi):
        def block(b, _):
            def body(cols):
                g, u = gu[b, 0, :, cols].astype(F32), gu[b, 1, :, cols].astype(F32)
                act[b, low, cols] = (g * jax.nn.sigmoid(g) * u).astype(BF)

            tiles(body)
            return 0

        lax.fori_loop(lo, hi, block, 0)

    def down(lo, hi, width):
        def body(i, _):
            cols = pl.ds(pl.multiple_of(i * width, width), width)
            a = jnp.concatenate([act[b, :, cols] for b in range(NZ)], axis=0)
            gdn[cols, :] = nn(a.astype(F32).T.astype(BF), og[...]).astype(BF)
            return 0

        lax.fori_loop(lo, hi, body, 0)

    def flip(b, _):
        for q in range(DB // 128):
            v = xa[rows(b), pl.ds(q * 128, 128)].astype(F32)
            xt[b, pl.ds(q * 128, 128), :] = v.T.astype(BF)
        return 0

    locals_[6].wait()
    make_terms([4])
    rs_step(1, True)
    ring_take(G, 2)
    make_terms([3, 5, 2, 6])
    rs_step(2, True)
    ring_take(U, 2)
    rs_step(2, False)
    locals_[5].wait()
    send_own(*xx)
    make_terms([1, 7, 0])
    rs_step(3, False)
    rs_step(4, False)
    ring_take(G, 3)
    ring_take(U, 3)
    pass_on(1, NCHIP, *xx)

    for d in (0, 1):
        for q in (0, 1):
            rs_copy(d, 4, q).wait_recv()

    def own_up(cols):
        t = terms[0, low, cols] + rs_in[0, 3, low, cols].astype(F32) + rs_in[1, 3, low, cols].astype(F32)
        up[z, :, cols] = t.astype(BF)

    tiles(own_up)
    ring_send(UP)
    for d in (0, 1):
        for q in (2, 3):
            rs_copy(d, 4, q).wait_recv()

    def own_deltas(cols):
        t = terms[0, high, cols] + rs_in[0, 3, high, cols].astype(F32) + rs_in[1, 3, high, cols].astype(F32)
        su, sg = silu_parts(gl[0, :, cols].astype(F32), gl[1, :, cols].astype(F32))
        dl[z, 0, high, cols] = (t * sg).astype(BF)
        dl[z, 1, high, cols] = (t * su).astype(BF)

    tiles(own_deltas)
    ring_send(GD)
    ring_send(UD)

    def deltas(blocks):
        for b in blocks:

            def body(cols, b=b):
                su, sg = silu_parts(gu[b, 0, :, cols].astype(F32), gu[b, 1, :, cols].astype(F32))
                t = up[b, :, cols].astype(F32)
                dl[b, 0, low, cols] = (t * sg).astype(BF)
                dl[b, 1, low, cols] = (t * su).astype(BF)

            tiles(body)

    wait_shared(xa, xc_s, xc_r)
    lax.fori_loop(0, NZ, flip, 0)
    locals_[7].wait()
    locals_[8].wait()

    def grads(blocks, first, last):
        def cat(vals, axis):
            return vals[0] if len(vals) == 1 else jnp.concatenate(vals, axis=axis)

        def body(i, _):
            r = pl.ds(pl.multiple_of(i * 512, 512), 512)
            xb = cat([xt[b, r, :] for b in blocks], 1)
            for a in (0, 1):
                t = nn(xb, cat([dl[b, a] for b in blocks], 0))
                if not first:
                    t = t + acc[a, r, :]
                if last:
                    (stage_g, stage_u)[a][r, :] = t.astype(BF)
                else:
                    acc[a, r, :] = t
            return 0

        lax.fori_loop(0, DB // 512, body, 0)

    def core_copy(b):
        return remote(cs.at[b], cr.at[b], cs_s.at[b], cs_r.at[b], sib)

    def x_copy(b, dx):
        return remote(s1.at[b, dx], r1.at[b, dx], p1_s.at[b, dx], p1_r.at[b, dx], chip_dev(4 * dx))

    def inputs(blocks):
        gdb = jnp.concatenate([dl[b, 0] for b in blocks], axis=0) if len(blocks) > 1 else dl[blocks[0], 0]
        udb = jnp.concatenate([dl[b, 1] for b in blocks], axis=0) if len(blocks) > 1 else dl[blocks[0], 1]

        def body(i, _):
            n = pl.ds(pl.multiple_of(i * 256, 256), 256)
            t = nt(gdb, wg[n, :]) + nt(udb, wu[n, :])
            for m, b in enumerate(blocks):
                for e in (0, 1):
                    base = m * TB + e * 2 * PR
                    lo, hi = t[base : base + PR], t[base + PR : base + 2 * PR]
                    own[b, i, pl.ds(e * PR, PR), :] = jnp.where(core == 0, lo, hi)
                    cs[b, i, pl.ds(e * PR, PR), :] = jnp.where(core == 0, hi, lo).astype(BF)
            return 0

        lax.fori_loop(0, DB // 256, body, 0)
        for b in blocks:
            core_copy(b).start()

    def sum_cores(blocks):
        for b in blocks:
            core_copy(b).wait_recv()
            for dx in (1, 2, 3, 0):
                i = lax.rem(cx + dx, 4)
                t = own[b, i] + cr[b, i].astype(F32)
                if dx == 0:
                    own[b, i] = t
                else:
                    s1[b, dx] = t.astype(BF)
                    x_copy(b, dx).start()

    def reduce_copy(b, e, j):
        return remote(
            s2.at[b, pl.ds(e * PR, PR)], rr.at[j], rr_s.at[j], rr_r.at[j], (z, 2 * (2 * b + e) + core)
        )

    def sum_x(blocks):
        for b in blocks:
            t = own[b, cx]
            for dx in (1, 2, 3):
                x_copy(b, dx).wait_recv()
                t = t + r1[b, dx].astype(F32)
            own[b, cx] = t
            s2[b] = t.astype(BF)
            for e in (0, 1):
                c = 2 * b + e

                @pl.when(c != chip)
                def _(b=b, e=e, c=c):
                    reduce_copy(b, e, lax.rem(c - chip + NCHIP, NCHIP)).start()

    def step_blocks(s):
        return [z] if s == 0 else [zrel(4)] if s == 4 else [zrel(-s), zrel(s)]

    deltas(step_blocks(0))
    inputs(step_blocks(0))
    ring_take(UP, 1)
    grads(step_blocks(0), True, False)
    ring_take(GD, 1)
    sum_cores(step_blocks(0))
    ring_take(UD, 1)
    for s in (1, 2, 3):
        now, before = step_blocks(s), step_blocks(s - 1)
        deltas(now)
        inputs(now)
        ring_take(UP, s + 1)
        grads(now, False, False)
        ring_take(GD, s + 1)
        sum_x(before)
        sum_cores(now)
        ring_take(UD, s + 1)
        if s == 1:
            ring_take(G, 4)
            ring_take(U, 4)
            all_act(0, 8)
        if s == 2:
            ring_take(ACT, 2)
    now = step_blocks(4)
    deltas(now)
    inputs(now)
    ring_take(ACT, 3)
    sum_x(step_blocks(3))
    sum_cores(now)
    grads(now, False, True)
    sum_x(now)
    ring_take(ACT, 4)
    down(0, 3, 256)
    down(6, 7, 128)

    def arrive(j, _):
        remote(s2.at[0, pl.ds(0, PR)], rr.at[j], rr_s.at[j], rr_r.at[j], sib).wait_recv()
        return 0

    lax.fori_loop(1, NCHIP, arrive, 0)
    rr[0] = own[chip // 2, cx, pl.ds(pl.multiple_of(lax.rem(chip, 2) * PR, PR), PR), :].astype(BF)
    for q in range(4):
        t = jnp.zeros((PR, 256), F32)
        for yy in range(4):
            t = t + rr[lax.rem(chip - (4 * q + yy) + NCHIP, NCHIP)].astype(F32)
        gi[:, q * 256 : (q + 1) * 256] = t.astype(BF)

    def gone(j, _):
        remote(og_rows(0, 0, 0), og_rows(0, 0, 0), og_s.at[0, j], og_r.at[0, j], sib).wait_send()
        remote(og_rows(0, 0, 0), og_rows(0, 0, 0), og_s.at[1, j], og_r.at[1, j], sib).wait_send()
        spread(xa, j, x_s, x_r).wait_send()
        remote(s2.at[0, pl.ds(0, PR)], rr.at[j], rr_s.at[j], rr_r.at[j], sib).wait_send()
        return 0

    lax.fori_loop(1, NCHIP, gone, 0)

    def gone_core(j, _):
        remote(og.at[mine], og.at[mine], ogc_s.at[j], ogc_r.at[j], sib).wait_send()
        share(xa, j, xc_s, xc_r).wait_send()
        return 0

    lax.fori_loop(0, NCHIP, gone_core, 0)

    def gone_block(b, _):
        core_copy(b).wait_send()
        for dx in (1, 2, 3):
            x_copy(b, dx).wait_send()
        return 0

    lax.fori_loop(0, NZ, gone_block, 0)
    for d in (0, 1):
        for i in range(6):
            for s in range(1, hops(d, i) + 1):
                ring_copy(i, d, s, 0).wait_send()
        for q in range(4):
            for s in range(1 if q // 2 == d else 2, 5):
                rs_copy(d, s, q).wait_send()


def write_out(*refs):
    sems = refs[8]
    copies = [pltpu.make_async_copy(refs[i], refs[4 + i], sems.at[i]) for i in range(4)]
    for c in copies:
        c.start()
    for c in copies:
        c.wait()


def on_device(block_input, output_grad, gate_pre, up_pre, w_gate, w_up, w_down):
    dma = pltpu.SemaphoreType.DMA
    any_ = pl.BlockSpec(memory_space=pl.ANY)
    plane = [dma((NCHIP,))] * 2
    shapes = ((PR, DB), (DB, FB), (DB, FB), (FB, DB))
    vmem = pl.BlockSpec(memory_space=pltpu.VMEM)
    held = pl.pallas_call(
        kernel,
        out_shape=tuple(pltpu.VMEM(s, BF) for s in shapes),
        in_specs=[any_] * 7,
        out_specs=(vmem,) * 4,
        scratch_shapes=[
            pltpu.VMEM((1024, DB), BF),
            pltpu.VMEM((1024, DB), BF),
            pltpu.VMEM((NZ, DB, TB), BF),
            pltpu.VMEM((NZ, 2, HT, FB), BF),
            pltpu.VMEM((2, HT, FB), BF),
            pltpu.VMEM((DB, FB), BF),
            pltpu.VMEM((DB, FB), BF),
            pltpu.VMEM((FB, DB), BF),
            pltpu.VMEM((NZ, TB, FB), BF),
            pltpu.VMEM((NZ, HT, FB), BF),
            pltpu.VMEM((NZ, 2, TB, FB), BF),
            pltpu.VMEM((NZ, TB, FB), F32),
            pltpu.VMEM((2, 4, TB, FB), BF),
            pltpu.VMEM((2, 4, TB, FB), BF),
            pltpu.VMEM((2, DB, FB), F32),
            pltpu.VMEM((NZ, 4, 2 * PR, 256), F32),
            pltpu.VMEM((NZ, 4, 2 * PR, 256), BF),
            pltpu.VMEM((NZ, 4, 2 * PR, 256), BF),
            pltpu.VMEM((NZ, 4, 2 * PR, 256), BF),
            pltpu.VMEM((NZ, 4, 2 * PR, 256), BF),
            pltpu.VMEM((NZ, 2 * PR, 256), BF),
            pltpu.VMEM((NCHIP, PR, 256), BF),
            dma((9,)),
            *[dma((6, 2, 4))] * 2,
            *[dma((2, NCHIP))] * 2, *plane,
            *plane, *plane,
            *[dma((2, 4, 4))] * 2,
            *[dma((NZ,))] * 2,
            *[dma((NZ, 4))] * 2,
            *plane,
        ],
        compiler_params=pltpu.CompilerParams(
            collective_id=0, has_side_effects=True, vmem_limit_bytes=56 * 2**20
        ),
        name="ffn_grad",
    )(block_input, output_grad, gate_pre, up_pre, w_gate, w_up, w_down)
    return pl.pallas_call(
        write_out,
        out_shape=tuple(jax.ShapeDtypeStruct(s, BF) for s in shapes),
        in_specs=[vmem] * 4,
        out_specs=(any_,) * 4,
        scratch_shapes=[dma((4,))],
        compiler_params=pltpu.CompilerParams(vmem_limit_bytes=2**20),
        name="write_out",
    )(*held)


def solution(mesh):
    return jax.shard_map(
        on_device,
        mesh=mesh,
        in_specs=(
            P("col", "row"),
            P("col", "row"),
            P("row", "col"),
            P("row", "col"),
            P("row", "col"),
            P("row", "col"),
            P("col", "row"),
        ),
        out_specs=(P("col", "row"), P("row", "col"), P("row", "col"), P("col", "row")),
        check_vma=False,
    )
```

```python
import functools

import jax
import jax.numpy as jnp
from jax import lax
from jax.experimental import pallas as pl
from jax.experimental.pallas import tpu as pltpu
from jax.sharding import PartitionSpec as P

MESH = pl.DeviceIdType.MESH
BF, F32 = jnp.bfloat16, jnp.float32
NZ, NCHIP = 8, 16
TB = 128
HT = 64
DB = 1024
FB = 896
PR = 32


def nt(a, b):
    return lax.dot_general(a, b, (((1,), (1,)), ((), ())), preferred_element_type=F32)


def nn(a, b):
    return lax.dot_general(a, b, (((1,), (0,)), ((), ())), preferred_element_type=F32)


def kernel(
    x_h, og_h, g_h, u_h, wg_h, wu_h, wd_h,
    gi, stage_g, stage_u, gdn,
    og, xa, xt, gu, gl, wg, wu, wd, act, up, dl, terms, rs_out, rs_in, acc, own, cs, cr, s1, r1, s2, rr,
    loc, ring_s, ring_r, og_s, og_r, ogc_s, ogc_r, x_s, x_r, xc_s, xc_r, rs_s, rs_r, cs_s, cs_r, p1_s, p1_r, rr_s, rr_r,
):
    z, col = lax.axis_index("row"), lax.axis_index("col")
    chip, core = col // 2, lax.rem(col, 2)
    cx, cy = chip // 4, lax.rem(chip, 4)
    sib = (z, col + 1 - 2 * core)

    def zdev(d):
        return (lax.rem(z + (1 if d == 0 else NZ - 1), NZ), col)

    def zrel(n):
        return lax.rem(z + (n % NZ), NZ)

    def chip_at(j):
        return lax.rem(chip + j + NCHIP, NCHIP)

    def chip_dev(j):
        return (z, 2 * chip_at(j) + core)

    def remote(src, dst, ss, rs, dev):
        return pltpu.make_async_remote_copy(
            src_ref=src, dst_ref=dst, send_sem=ss, recv_sem=rs, device_id=dev, device_id_type=MESH
        )

    mine = pl.ds(pl.multiple_of(col * PR, PR), PR)
    locals_ = [
        pltpu.make_async_copy(g_h.at[pl.ds(0, HT)], gu.at[z, 0], loc.at[0]),
        pltpu.make_async_copy(u_h.at[pl.ds(0, HT)], gu.at[z, 1], loc.at[1]),
        pltpu.make_async_copy(og_h, og.at[mine], loc.at[2]),
        pltpu.make_async_copy(g_h.at[pl.ds(HT, HT)], gl.at[0], loc.at[3]),
        pltpu.make_async_copy(u_h.at[pl.ds(HT, HT)], gl.at[1], loc.at[4]),
        pltpu.make_async_copy(x_h, xa.at[mine], loc.at[5]),
        pltpu.make_async_copy(wd_h, wd, loc.at[6]),
        pltpu.make_async_copy(wg_h, wg, loc.at[7]),
        pltpu.make_async_copy(wu_h, wu, loc.at[8]),
    ]
    for c in locals_:
        c.start()

    bar = pltpu.get_barrier_semaphore()
    for d in (0, 1):
        pl.semaphore_signal(bar, inc=1, device_id=zdev(d), device_id_type=MESH)
    pl.semaphore_signal(bar, inc=1, device_id=sib, device_id_type=MESH)

    def greet(j, _):
        pl.semaphore_signal(bar, inc=1, device_id=chip_dev(j), device_id_type=MESH)
        return 0

    lax.fori_loop(1, NCHIP, greet, 0)
    pl.semaphore_wait(bar, NCHIP + 2)

    def piece(buf, j):
        return buf.at[pl.ds(pl.multiple_of((2 * chip_at(j) + core) * PR, PR), PR)]

    def spread(buf, j, ss, rs):
        return remote(buf.at[mine], buf.at[mine], ss.at[j], rs.at[j], chip_dev(j))

    def landed(buf, j, ss, rs):
        p = piece(buf, NCHIP - j)
        return remote(p, p, ss.at[j], rs.at[j], chip_dev(j))

    def share(buf, j, ss, rs):
        p = piece(buf, NCHIP - j)
        return remote(p, p, ss.at[j], rs.at[j], sib)

    def shared(buf, j, ss, rs):
        p = buf.at[pl.ds(pl.multiple_of((2 * chip_at(NCHIP - j) + 1 - core) * PR, PR), PR)]
        return remote(p, p, ss.at[j], rs.at[j], sib)

    def send_own(buf, s, r, cs_, cr_):
        def body(j, _):
            spread(buf, j, s, r).start()
            return 0

        lax.fori_loop(1, NCHIP, body, 0)
        share(buf, 0, cs_, cr_).start()

    def pass_on(lo, hi, buf, s, r, cs_, cr_):
        def body(j, _):
            landed(buf, j, s, r).wait_recv()
            share(buf, j, cs_, cr_).start()
            return 0

        lax.fori_loop(lo, hi, body, 0)

    def wait_shared(buf, cs_, cr_):
        def body(j, _):
            shared(buf, j, cs_, cr_).wait_recv()
            return 0

        lax.fori_loop(0, NCHIP, body, 0)

    xx = (xa, x_s, x_r, xc_s, xc_r)

    def chip_xy(dx, dy):
        return lax.rem(cx + dx + 4, 4) * 4 + lax.rem(cy + dy + 4, 4)

    def og_rows(dx, dy, h):
        return og.at[pl.ds(pl.multiple_of((2 * chip_xy(-dx, -dy) + core) * PR + h * 16, 16), 16)]

    def og_copy(h, dx, dy):
        if h == 0:
            p, to = og_rows(dx if dy else 0, 0, 0), (0, dy) if dy else (dx, 0)
        else:
            p, to = og_rows(0, dy if dx else 0, 1), (dx, 0) if dx else (0, dy)
        j = 4 * dx + dy
        return remote(p, p, og_s.at[h, j], og_r.at[h, j], (z, 2 * chip_xy(*to) + core))

    def og_wait(h, dx, dy):
        p, j = og_rows(dx, dy, h), 4 * dx + dy
        remote(p, p, og_s.at[h, j], og_r.at[h, j], sib).wait_recv()

    def og_share(dx, dy, their):
        c = 2 * chip_xy(-dx, -dy) + (1 - core if their else core)
        p, j = og.at[pl.ds(pl.multiple_of(c * PR, PR), PR)], 4 * dx + dy
        return remote(p, p, ogc_s.at[j], ogc_r.at[j], sib)

    FAR = (1, 3, 2)
    OFFSETS = [(dx, dy) for dx in range(4) for dy in range(4)]

    def og_start():
        for n in FAR:
            og_copy(0, n, 0).start()
            og_copy(1, 0, n).start()
        og_share(0, 0, False).start()
        for n in FAR:
            og_copy(0, 0, n).start()
            og_copy(1, n, 0).start()

    def og_turn():
        for n in FAR:
            og_wait(0, n, 0)
            for m in FAR:
                og_copy(0, n, m).start()
            og_wait(1, 0, n)
            for m in FAR:
                og_copy(1, m, n).start()

    def og_finish(offsets):
        for dx, dy in offsets:
            if dy:
                og_wait(0, dx, dy)
            if dx:
                og_wait(1, dx, dy)
            if dx or dy:
                og_share(dx, dy, False).start()


    G, U, UP, GD, UD, ACT = range(6)
    low, high = pl.ds(0, HT), pl.ds(HT, HT)

    def ring_ref(i, n):
        b = zrel(n)
        return (
            lambda: gu.at[b, 0],
            lambda: gu.at[b, 1],
            lambda: up.at[b],
            lambda: dl.at[b, 0, high],
            lambda: dl.at[b, 1, high],
            lambda: act.at[b, high],
        )[i]()

    LONG = (0, 1, 1, 0, 1, 0)

    def hops(d, i):
        return 4 if LONG[i] == d else 3

    def ring_copy(i, d, s, n):
        p = ring_ref(i, n)
        return remote(p, p, ring_s.at[i, d, s - 1], ring_r.at[i, d, s - 1], zdev(d))

    def ring_send(i):
        for d in (LONG[i], 1 - LONG[i]):
            ring_copy(i, d, 1, 0).start()

    def ring_take(i, s):
        for d in (LONG[i], 1 - LONG[i]):
            if s <= hops(d, i):
                n = -s if d == 0 else s
                ring_copy(i, d, s, n).wait_recv()
                if s + 1 <= hops(d, i):
                    ring_copy(i, d, s + 1, n).start()

    locals_[0].wait()
    ring_send(G)
    locals_[1].wait()
    ring_send(U)
    locals_[2].wait()
    og_start()

    def silu_parts(g, u):
        s = jax.nn.sigmoid(g)
        return g * s, u * s * (1.0 + g * (1.0 - s))

    def tiles(body):
        def step(q, _):
            body(pl.ds(pl.multiple_of(q * 128, 128), 128))
            return 0

        lax.fori_loop(0, FB // 128, step, 0)

    locals_[3].wait()
    locals_[4].wait()

    def own_act(cols):
        g, u = gl[0, :, cols].astype(F32), gl[1, :, cols].astype(F32)
        act[z, high, cols] = (g * jax.nn.sigmoid(g) * u).astype(BF)

    tiles(own_act)

    ring_send(ACT)
    og_turn()
    ring_take(G, 1)
    ring_take(U, 1)
    og_finish(OFFSETS[:8])
    ring_take(ACT, 1)
    og_finish(OFFSETS[8:])
    for n in OFFSETS:
        og_share(*n, True).wait_recv()

    def rows(b):
        return pl.ds(pl.multiple_of(b * TB, TB), TB)

    def make_terms(rels):
        a = jnp.concatenate([og[rows(zrel(r)), :] for r in rels], axis=0) if len(rels) > 1 else og[rows(zrel(rels[0])), :]

        def tile(lanes):
            t = nt(a, wd[lanes, :])
            for n, r in enumerate(rels):
                terms[r, :, lanes] = t[n * TB : (n + 1) * TB].astype(BF).astype(F32)

        def body(i, _):
            tile(pl.ds(pl.multiple_of(i * 256, 256), 256))
            return 0

        lax.fori_loop(0, 3, body, 0)
        tile(pl.ds(768, 128))

    QT = TB // 4

    def rs_copy(d, s, q):
        r = pl.ds(q * QT, QT)
        return remote(
            rs_out.at[d, s - 1, r], rs_in.at[d, s - 1, r], rs_s.at[d, s - 1, q], rs_r.at[d, s - 1, q], zdev(d)
        )

    def rs_step(s, fresh):
        for o in (2, 3, 0, 1):
            for d in (0, 1):
                q = o ^ (2 * d)
                first = 1 if o < 2 else 2
                if s < first or (s == first) != fresh:
                    continue
                r = pl.ds(q * QT, QT)
                t = terms[5 - s if d == 0 else 3 + s, r, :]
                if not fresh:
                    rs_copy(d, s - 1, q).wait_recv()
                    t = t + rs_in[d, s - 2, r, :].astype(F32)
                rs_out[d, s - 1, r, :] = t.astype(BF)
                rs_copy(d, s, q).start()

    def all_act(lo, hi):
        def block(b, _):
            def body(cols):
                g, u = gu[b, 0, :, cols].astype(F32), gu[b, 1, :, cols].astype(F32)
                act[b, low, cols] = (g * jax.nn.sigmoid(g) * u).astype(BF)

            tiles(body)
            return 0

        lax.fori_loop(lo, hi, block, 0)

    def down(lo, hi, width):
        def body(i, _):
            cols = pl.ds(pl.multiple_of(i * width, width), width)
            a = jnp.concatenate([act[b, :, cols] for b in range(NZ)], axis=0)
            gdn[cols, :] = nn(a.astype(F32).T.astype(BF), og[...]).astype(BF)
            return 0

        lax.fori_loop(lo, hi, body, 0)

    def flip(b, _):
        for q in range(DB // 128):
            v = xa[rows(b), pl.ds(q * 128, 128)].astype(F32)
            xt[b, pl.ds(q * 128, 128), :] = v.T.astype(BF)
        return 0

    locals_[6].wait()
    make_terms([4])
    rs_step(1, True)
    ring_take(G, 2)
    make_terms([3, 5, 2, 6])
    rs_step(2, True)
    ring_take(U, 2)
    rs_step(2, False)
    locals_[5].wait()
    send_own(*xx)
    make_terms([1, 7, 0])
    rs_step(3, False)
    rs_step(4, False)
    ring_take(G, 3)
    ring_take(U, 3)
    pass_on(1, NCHIP, *xx)

    for d in (0, 1):
        for q in (0, 1):
            rs_copy(d, 4, q).wait_recv()

    def own_up(cols):
        t = terms[0, low, cols] + rs_in[0, 3, low, cols].astype(F32) + rs_in[1, 3, low, cols].astype(F32)
        up[z, :, cols] = t.astype(BF)

    tiles(own_up)
    ring_send(UP)
    for d in (0, 1):
        for q in (2, 3):
            rs_copy(d, 4, q).wait_recv()

    def own_deltas(cols):
        t = terms[0, high, cols] + rs_in[0, 3, high, cols].astype(F32) + rs_in[1, 3, high, cols].astype(F32)
        su, sg = silu_parts(gl[0, :, cols].astype(F32), gl[1, :, cols].astype(F32))
        dl[z, 0, high, cols] = (t * sg).astype(BF)
        dl[z, 1, high, cols] = (t * su).astype(BF)

    tiles(own_deltas)
    ring_send(GD)
    ring_send(UD)

    def deltas(blocks):
        for b in blocks:

            def body(cols, b=b):
                su, sg = silu_parts(gu[b, 0, :, cols].astype(F32), gu[b, 1, :, cols].astype(F32))
                t = up[b, :, cols].astype(F32)
                dl[b, 0, low, cols] = (t * sg).astype(BF)
                dl[b, 1, low, cols] = (t * su).astype(BF)

            tiles(body)

    wait_shared(xa, xc_s, xc_r)
    lax.fori_loop(0, NZ, flip, 0)
    locals_[7].wait()
    locals_[8].wait()

    def grads(blocks, first, last):
        def cat(vals, axis):
            return vals[0] if len(vals) == 1 else jnp.concatenate(vals, axis=axis)

        def body(i, _):
            r = pl.ds(pl.multiple_of(i * 512, 512), 512)
            xb = cat([xt[b, r, :] for b in blocks], 1)
            for a in (0, 1):
                t = nn(xb, cat([dl[b, a] for b in blocks], 0))
                if not first:
                    t = t + acc[a, r, :]
                if last:
                    (stage_g, stage_u)[a][r, :] = t.astype(BF)
                else:
                    acc[a, r, :] = t
            return 0

        lax.fori_loop(0, DB // 512, body, 0)

    def core_copy(b):
        return remote(cs.at[b], cr.at[b], cs_s.at[b], cs_r.at[b], sib)

    def x_copy(b, dx):
        return remote(s1.at[b, dx], r1.at[b, dx], p1_s.at[b, dx], p1_r.at[b, dx], chip_dev(4 * dx))

    def inputs(blocks):
        gdb = jnp.concatenate([dl[b, 0] for b in blocks], axis=0) if len(blocks) > 1 else dl[blocks[0], 0]
        udb = jnp.concatenate([dl[b, 1] for b in blocks], axis=0) if len(blocks) > 1 else dl[blocks[0], 1]

        def body(i, _):
            n = pl.ds(pl.multiple_of(i * 256, 256), 256)
            t = nt(gdb, wg[n, :]) + nt(udb, wu[n, :])
            for m, b in enumerate(blocks):
                for e in (0, 1):
                    base = m * TB + e * 2 * PR
                    lo, hi = t[base : base + PR], t[base + PR : base + 2 * PR]
                    own[b, i, pl.ds(e * PR, PR), :] = jnp.where(core == 0, lo, hi)
                    cs[b, i, pl.ds(e * PR, PR), :] = jnp.where(core == 0, hi, lo).astype(BF)
            return 0

        lax.fori_loop(0, DB // 256, body, 0)
        for b in blocks:
            core_copy(b).start()

    def sum_cores(blocks):
        for b in blocks:
            core_copy(b).wait_recv()
            for dx in (1, 2, 3, 0):
                i = lax.rem(cx + dx, 4)
                t = own[b, i] + cr[b, i].astype(F32)
                if dx == 0:
                    own[b, i] = t
                else:
                    s1[b, dx] = t.astype(BF)
                    x_copy(b, dx).start()

    def reduce_copy(b, e, j):
        return remote(
            s2.at[b, pl.ds(e * PR, PR)], rr.at[j], rr_s.at[j], rr_r.at[j], (z, 2 * (2 * b + e) + core)
        )

    def sum_x(blocks):
        for b in blocks:
            t = own[b, cx]
            for dx in (1, 2, 3):
                x_copy(b, dx).wait_recv()
                t = t + r1[b, dx].astype(F32)
            own[b, cx] = t
            s2[b] = t.astype(BF)
            for e in (0, 1):
                c = 2 * b + e

                @pl.when(c != chip)
                def _(b=b, e=e, c=c):
                    reduce_copy(b, e, lax.rem(c - chip + NCHIP, NCHIP)).start()

    def step_blocks(s):
        return [z] if s == 0 else [zrel(4)] if s == 4 else [zrel(-s), zrel(s)]

    deltas(step_blocks(0))
    inputs(step_blocks(0))
    ring_take(UP, 1)
    grads(step_blocks(0), True, False)
    ring_take(GD, 1)
    sum_cores(step_blocks(0))
    ring_take(UD, 1)
    for s in (1, 2, 3):
        now, before = step_blocks(s), step_blocks(s - 1)
        deltas(now)
        inputs(now)
        ring_take(UP, s + 1)
        grads(now, False, False)
        ring_take(GD, s + 1)
        sum_x(before)
        sum_cores(now)
        ring_take(UD, s + 1)
        if s == 1:
            ring_take(G, 4)
            ring_take(U, 4)
            all_act(0, 8)
        if s == 2:
            ring_take(ACT, 2)
    now = step_blocks(4)
    deltas(now)
    inputs(now)
    sum_cores(now)
    sum_x(step_blocks(3))
    ring_take(ACT, 3)
    grads(now, False, True)
    sum_x(now)
    ring_take(ACT, 4)
    down(0, 3, 256)
    down(6, 7, 128)

    def arrive(j, _):
        remote(s2.at[0, pl.ds(0, PR)], rr.at[j], rr_s.at[j], rr_r.at[j], sib).wait_recv()
        return 0

    lax.fori_loop(1, NCHIP, arrive, 0)
    rr[0] = own[chip // 2, cx, pl.ds(pl.multiple_of(lax.rem(chip, 2) * PR, PR), PR), :].astype(BF)
    for q in range(4):
        t = jnp.zeros((PR, 256), F32)
        for yy in range(4):
            t = t + rr[lax.rem(chip - (4 * q + yy) + NCHIP, NCHIP)].astype(F32)
        gi[:, q * 256 : (q + 1) * 256] = t.astype(BF)

    def gone(j, _):
        remote(og_rows(0, 0, 0), og_rows(0, 0, 0), og_s.at[0, j], og_r.at[0, j], sib).wait_send()
        remote(og_rows(0, 0, 0), og_rows(0, 0, 0), og_s.at[1, j], og_r.at[1, j], sib).wait_send()
        spread(xa, j, x_s, x_r).wait_send()
        remote(s2.at[0, pl.ds(0, PR)], rr.at[j], rr_s.at[j], rr_r.at[j], sib).wait_send()
        return 0

    lax.fori_loop(1, NCHIP, gone, 0)

    def gone_core(j, _):
        remote(og.at[mine], og.at[mine], ogc_s.at[j], ogc_r.at[j], sib).wait_send()
        share(xa, j, xc_s, xc_r).wait_send()
        return 0

    lax.fori_loop(0, NCHIP, gone_core, 0)

    def gone_block(b, _):
        core_copy(b).wait_send()
        for dx in (1, 2, 3):
            x_copy(b, dx).wait_send()
        return 0

    lax.fori_loop(0, NZ, gone_block, 0)
    for d in (0, 1):
        for i in range(6):
            for s in range(1, hops(d, i) + 1):
                ring_copy(i, d, s, 0).wait_send()
        for q in range(4):
            for s in range(1 if q // 2 == d else 2, 5):
                rs_copy(d, s, q).wait_send()


def write_out(*refs):
    sems = refs[8]
    copies = [pltpu.make_async_copy(refs[i], refs[4 + i], sems.at[i]) for i in range(4)]
    for c in copies:
        c.start()
    for c in copies:
        c.wait()


def on_device(block_input, output_grad, gate_pre, up_pre, w_gate, w_up, w_down):
    dma = pltpu.SemaphoreType.DMA
    any_ = pl.BlockSpec(memory_space=pl.ANY)
    plane = [dma((NCHIP,))] * 2
    shapes = ((PR, DB), (DB, FB), (DB, FB), (FB, DB))
    vmem = pl.BlockSpec(memory_space=pltpu.VMEM)
    held = pl.pallas_call(
        kernel,
        out_shape=tuple(pltpu.VMEM(s, BF) for s in shapes),
        in_specs=[any_] * 7,
        out_specs=(vmem,) * 4,
        scratch_shapes=[
            pltpu.VMEM((1024, DB), BF),
            pltpu.VMEM((1024, DB), BF),
            pltpu.VMEM((NZ, DB, TB), BF),
            pltpu.VMEM((NZ, 2, HT, FB), BF),
            pltpu.VMEM((2, HT, FB), BF),
            pltpu.VMEM((DB, FB), BF),
            pltpu.VMEM((DB, FB), BF),
            pltpu.VMEM((FB, DB), BF),
            pltpu.VMEM((NZ, TB, FB), BF),
            pltpu.VMEM((NZ, HT, FB), BF),
            pltpu.VMEM((NZ, 2, TB, FB), BF),
            pltpu.VMEM((NZ, TB, FB), F32),
            pltpu.VMEM((2, 4, TB, FB), BF),
            pltpu.VMEM((2, 4, TB, FB), BF),
            pltpu.VMEM((2, DB, FB), F32),
            pltpu.VMEM((NZ, 4, 2 * PR, 256), F32),
            pltpu.VMEM((NZ, 4, 2 * PR, 256), BF),
            pltpu.VMEM((NZ, 4, 2 * PR, 256), BF),
            pltpu.VMEM((NZ, 4, 2 * PR, 256), BF),
            pltpu.VMEM((NZ, 4, 2 * PR, 256), BF),
            pltpu.VMEM((NZ, 2 * PR, 256), BF),
            pltpu.VMEM((NCHIP, PR, 256), BF),
            dma((9,)),
            *[dma((6, 2, 4))] * 2,
            *[dma((2, NCHIP))] * 2, *plane,
            *plane, *plane,
            *[dma((2, 4, 4))] * 2,
            *[dma((NZ,))] * 2,
            *[dma((NZ, 4))] * 2,
            *plane,
        ],
        compiler_params=pltpu.CompilerParams(
            collective_id=0, has_side_effects=True, vmem_limit_bytes=56 * 2**20
        ),
        name="ffn_grad",
    )(block_input, output_grad, gate_pre, up_pre, w_gate, w_up, w_down)
    return pl.pallas_call(
        write_out,
        out_shape=tuple(jax.ShapeDtypeStruct(s, BF) for s in shapes),
        in_specs=[vmem] * 4,
        out_specs=(any_,) * 4,
        scratch_shapes=[dma((4,))],
        compiler_params=pltpu.CompilerParams(vmem_limit_bytes=2**20),
        name="write_out",
    )(*held)


def solution(mesh):
    return jax.shard_map(
        on_device,
        mesh=mesh,
        in_specs=(
            P("col", "row"),
            P("col", "row"),
            P("row", "col"),
            P("row", "col"),
            P("row", "col"),
            P("row", "col"),
            P("col", "row"),
        ),
        out_specs=(P("col", "row"), P("row", "col"), P("row", "col"), P("col", "row")),
        check_vma=False,
    )
```
